256 devices in a mesh: dp: 32 (over y, z_hi, core), mp: 8 (over z_lo, x).
Axes of the slice: x: 4, y: 4, z: 8 (z_hi: 4, z_lo: 2; z = z_hi * 2 + z_lo), core: 2. Of those that a mesh axis runs over, the one named last changes fastest.
Arguments:
- inputs: bfloat16 [4, 8192, 4096], P(None, 'dp'), may hold values from -60 to 60
- gate_cotangent: bfloat16 [4, 8192, 6144], P(None, 'dp', 'mp'), may hold values from -6 to 6
- ff_blocks: int32 [4], replicated, may hold values from 24 to 48, as said below
- layer_active: int32 [4], replicated, may hold values from 0 to 1, as said below
- param: float32 [4096, 6144], P(('dp', 'mp')), may hold values from -0.09375 to 0.09375
- moment: float32 [4096, 6144], P(('dp', 'mp')), may hold values from -3 to 3
- second_moment: float32 [4096, 6144], P(('dp', 'mp')), may hold values from 0.5 to 2
Outputs:
- new_param: float32 [4096, 6144], P(('dp', 'mp'))
- new_moment: float32 [4096, 6144], P(('dp', 'mp'))
- new_second: float32 [4096, 6144], P(('dp', 'mp'))
The draws below stay inside these ranges and needn't reach their ends.
Inputs may be any that keep to these rules, and one draw needn't show every extreme that they name: `ff_blocks`: entry 0 is 6144 // 128 (the largest subnet), entry 1 is 6144 // (256) (the smallest). `layer_active`: entry 0 is 1, and exactly one of entries 1, 2 and 3 is 0.
All inputs are finite; a program needn't handle non-finite values.
Results may differ from the reference program's by a relative error of at most 0.0003.
Values sent between devices are 32-bit elements; how exact they have to be, the bound alone decides.
No kernel may reach another device: no remote copies, remote signals or barrier semaphores. Data moves between devices by JAX's collectives and lax.ppermute only.
A program may use at most 128 MiB of HBM per device.

```python
import math
import jax
import jax.numpy as jnp
from jax import lax

D = 4096
FF = 6144
BLOCK = 128
SUBNETS = 4
STEP = 10
TOK_DEV = 256
TOKENS = 8192


def draw_inputs(key, part):
    base = jnp.clip(jax.random.normal(jax.random.fold_in(key, 5), (SUBNETS, TOKENS, D), jnp.float32), -4.0, 4.0)
    column = lax.broadcasted_iota(jnp.int32, (D,), 0)
    place = column.astype(jnp.float32) / D
    scale = 1.0 + 2.0 * place
    replicas = TOKENS // TOK_DEV
    order = jax.random.permutation(jax.random.fold_in(key, 7), replicas).astype(jnp.int32)
    owner = lax.broadcasted_iota(jnp.int32, (TOKENS,), 0) // TOK_DEV
    paired = order[owner]
    column_block = column // (D // replicas)
    boost = jnp.where(column_block[None, :] == paired[:, None], 3.0, 1.0)
    return (base * scale[None, None, :] * boost[None, :, :]).astype(jnp.bfloat16)


def draw_ff_blocks(key, part):
    most = FF // BLOCK
    half = most // 2
    first = jax.random.randint(jax.random.fold_in(key, 11), (1,), half, most + 1)
    second = jax.random.randint(jax.random.fold_in(key, 13), (1,), half, most + 1)
    head = jnp.array([most, half], jnp.int32)
    return jnp.concatenate([head, first.astype(jnp.int32), second.astype(jnp.int32), jnp.full((SUBNETS - 4,), most, jnp.int32)]).astype(jnp.int32)


def draw_layer_active(key, part):
    pick = jax.random.randint(jax.random.fold_in(key, 23), (), 1, 4)
    index = lax.broadcasted_iota(jnp.int32, (SUBNETS,), 0)
    return jnp.where(index == pick, 0, 1).astype(jnp.int32)


def block_scale(stream_key, dims, shards, smallest, high):
    gain, own = 1.0, jax.random.fold_in(stream_key, 6)
    for dim, parts in shards:
        draws = jnp.exp(jax.random.uniform(jax.random.fold_in(own, dim), (parts,), jnp.float32, smallest / len(shards), high / len(shards)))
        gain = gain * jnp.repeat(draws, dims[dim] // parts).reshape([-1 if axis == dim else 1 for axis in range(len(dims))])
    return gain


def normal_values(rng, shape, width, limit, shards=(), held_as=jnp.bfloat16):
    values = width * jax.random.normal(rng, shape, jnp.float32)
    if shards:
        values = values * block_scale(rng, shape, shards, -0.22, 0.18)
    return jnp.clip(values, -limit, limit).astype(held_as)


def setup_inputs(seed: int = 0) -> dict:
    key_list = jax.random.split(jax.random.key(seed), 8)
    return {
        "inputs": draw_inputs(jax.random.fold_in(key_list[7], 71), 0),
        "gate_cotangent": normal_values(key_list[1], (SUBNETS, TOKENS, FF), 1.0, 6.0, ((1, 32), (2, 8))),
        "ff_blocks": draw_ff_blocks(jax.random.fold_in(key_list[7], 71), 0),
        "layer_active": draw_layer_active(jax.random.fold_in(key_list[7], 71), 0),
        "param": normal_values(key_list[4], (D, FF), D ** -0.5, 0.09375, ((0, 256),), jnp.float32),
        "moment": normal_values(key_list[5], (D, FF), 0.5, 3.0, ((0, 256),), jnp.float32),
        "second_moment": jnp.clip(jnp.exp(math.log(2.0) - 1.3862944 * jax.random.uniform(key_list[6], (D, FF), jnp.float32) ** block_scale(key_list[6], (D, FF), ((0, 256),), -0.2, 0.2)), 0.5, 2.0),
    }


def reference(inputs, gate_cotangent, ff_blocks, layer_active, param, moment, second_moment):
    column = lax.broadcasted_iota(jnp.int32, (SUBNETS, FF), 1)
    keep = (column < BLOCK * ff_blocks[:, None]) & (layer_active[:, None] == 1)
    masked = jnp.where(keep[:, None, :], gate_cotangent, jnp.zeros((), jnp.bfloat16))
    rows_in = inputs.reshape(SUBNETS * TOKENS, D)
    rows_ct = masked.reshape(SUBNETS * TOKENS, FF)
    gradient = lax.dot_general(rows_in, rows_ct, (((0,), (0,)), ((), ())), preferred_element_type=jnp.float32)
    total = jnp.sqrt(jnp.sum(gradient * gradient))
    factor = jnp.minimum(1.0, jnp.sqrt(1.0 * D * FF) / (total + 1e-06))
    clipped = gradient * factor
    new_moment = 0.9 * moment + 0.1 * clipped
    new_second = 0.95 * second_moment + 0.05 * clipped * clipped
    first_hat = new_moment / (1.0 - 0.9 ** STEP)
    second_hat = new_second / (1.0 - 0.95 ** STEP)
    new_param = param - 0.02 * (first_hat / (jnp.sqrt(second_hat) + 1e-08) + 0.1 * param)
    return (new_param, new_moment, new_second)
```

```python
import functools
import math

import jax
import jax.numpy as jnp
from jax import lax
from jax.experimental import pallas as pl
from jax.experimental.pallas import tpu as pltpu
from jax.sharding import Mesh
from jax.sharding import PartitionSpec as P

D = 4096
FF = 6144
BLOCK = 128
STEP = 10
LANES = 128
LIVE = 3
AXES = ("y", "z", "core", "z_lo", "x")
DP = ("y", "z", "core")
MP = ("z_lo", "x")
SIZES = {"y": 4, "z": 4, "core": 2, "z_lo": 2, "x": 4}

CHUNKS = (160, 144, 80)
STREAM_A = (("y", 1), ("z", 1), ("y", 3), ("z", 3))
STREAM_B = (("y", 3), ("z", 3), ("y", 1), ("z", 1))


def swap(value, axis, mask):
    return lax.ppermute(value, axis, [(i, i ^ mask) for i in range(SIZES[axis])])


def product_kernel(widths, tile_ref, live_ref, limit_ref, *refs):
    x_refs, m_refs = refs[: 4 * LIVE], refs[4 * LIVE : 5 * LIVE]
    outs, mt_ref = refs[5 * LIVE : -1], refs[-1]

    @pl.when(pl.program_id(0) == 0)
    def _():
        for s in range(LIVE):
            values = m_refs[s][0]
            column = lax.broadcasted_iota(jnp.int32, values.shape, 1)
            values = jnp.where(column < limit_ref[s], values, jnp.zeros_like(values))
            mt_ref[:, s * 256 : (s + 1) * 256] = values.T

    first = 0
    for k, width in enumerate(widths):
        rows = slice(first, first + width)
        total = None
        for s in range(LIVE):
            right = jnp.concatenate([x_refs[4 * s + t][0] for t in range(4)], axis=1)
            part = jnp.dot(
                mt_ref[rows, s * 256 : (s + 1) * 256], right, preferred_element_type=jnp.float32
            )
            total = part if total is None else total + part
        for half in range(2):
            low = half * (width // 2)
            for t in range(4):
                at = (t // 2, t % 2) if half == 0 else (t % 2, t // 2)
                outs[2 * k + half][0, at[0], 0, at[1]] = total[
                    low : low + width // 2, t * LANES : (t + 1) * LANES
                ]
        first += width


def product(tiles, live, limits, x, m, chunks):
    widths = tuple(2 * j for j in chunks)
    x_specs = [
        pl.BlockSpec((1, 256, LANES), lambda i, tile, lv, lim, s=s, t=t: (lv[s], 0, tile[4 * i + t]))
        for s in range(LIVE)
        for t in range(4)
    ]
    m_specs = [
        pl.BlockSpec((1, 256, m.shape[2]), lambda i, tile, lv, lim, s=s: (lv[s], 0, 0))
        for s in range(LIVE)
    ]
    out_shape, out_specs = [], []
    for j in chunks:
        for half in range(2):
            out_shape.append(jax.ShapeDtypeStruct((2, 2, 2, 2, j, LANES), jnp.float32))
            if half == 0:
                place = lambda i, tile, lv, lim: (i // 2, 0, i % 2, 0, 0, 0)
            else:
                place = lambda i, tile, lv, lim: (i % 2, 0, i // 2, 0, 0, 0)
            out_specs.append(pl.BlockSpec((1, 2, 1, 2, j, LANES), place))
    return pl.pallas_call(
        functools.partial(product_kernel, widths),
        grid_spec=pltpu.PrefetchScalarGridSpec(
            num_scalar_prefetch=3,
            grid=(4,),
            in_specs=x_specs + m_specs,
            out_specs=out_specs,
            scratch_shapes=[pltpu.VMEM((m.shape[2], LIVE * 256), jnp.bfloat16)],
        ),
        out_shape=out_shape,
        compiler_params=pltpu.CompilerParams(vmem_limit_bytes=24 * 1024 * 1024),
    )(tiles, live, limits, *([x] * (4 * LIVE)), *([m] * LIVE))


def reduce_stream(own, other, steps):
    parts = [own, other]
    for axis, mask in steps:
        send = sum(p[0] for p in parts[1:]) + parts[0][0]
        received = swap(send, axis, mask)
        parts = [p[1] for p in parts] + [received]
    return sum(parts[1:]) + parts[0]


def shards(inputs, gate_cotangent, ff_blocks, layer_active, param, moment, second_moment):
    y, z, core = (lax.axis_index(a) for a in DP)
    cols = gate_cotangent.shape[2]
    me = lax.axis_index(MP)
    index = jnp.arange(LIVE, dtype=jnp.int32)
    idle = jnp.sum(jnp.where(layer_active == 1, 0, jnp.arange(4, dtype=jnp.int32)))
    live = index + (index >= idle).astype(jnp.int32)
    limits = BLOCK * ff_blocks[live] - me * cols
    step = jnp.arange(4, dtype=jnp.int32)
    offset = (1 - step // 2) * 1 ^ (1 - step % 2) * 3
    tiles = (((y ^ offset)[:, None] * 4 + (z ^ offset)[None, :]) * 2).reshape(16)
    others = product(tiles + (1 - core), live, limits, inputs, gate_cotangent, CHUNKS)
    others = [swap(o, "core", 1) for o in others]
    owns = product(tiles + core, live, limits, inputs, gate_cotangent, CHUNKS)
    done = [
        reduce_stream(own, other, STREAM_A if n % 2 == 0 else STREAM_B)
        for n, (own, other) in enumerate(zip(owns, others))
    ]
    tile = jnp.concatenate(done, axis=0)
    squares = jnp.sum((tile * tile).reshape(-1, 8, LANES), axis=0)
    gradient = lax.all_to_all(tile.T, MP, split_axis=0, concat_axis=1, tiled=True)
    for axis, mask in (
        ("core", 1), ("y", 1), ("y", 3), ("x", 1), ("x", 3), ("z_lo", 1), ("z", 1), ("z", 3),
    ):
        squares = squares + swap(squares, axis, mask)
    total = jnp.sqrt(jnp.sum(squares))
    factor = jnp.minimum(1.0, math.sqrt(1.0 * D * FF) / (total + 1e-06))
    clipped = gradient * factor
    new_moment = 0.9 * moment + 0.1 * clipped
    new_second = 0.95 * second_moment + 0.05 * clipped * clipped
    first_hat = new_moment / (1.0 - 0.9**STEP)
    second_hat = new_second / (1.0 - 0.95**STEP)
    new_param = param - 0.02 * (first_hat / (jnp.sqrt(second_hat) + 1e-08) + 0.1 * param)
    return (new_param, new_moment, new_second)


def solution(mesh):
    split = Mesh(mesh.devices.reshape(4, 4, 2, 2, 4), AXES)
    rows = P(AXES, None)
    return jax.shard_map(
        shards,
        mesh=split,
        in_specs=(P(None, DP, None), P(None, DP, MP), P(), P(), rows, rows, rows),
        out_specs=(rows, rows, rows),
        check_vma=False,
    )
```

```python
import functools
import math

import jax
import jax.numpy as jnp
from jax import lax
from jax.experimental import pallas as pl
from jax.experimental.pallas import tpu as pltpu
from jax.sharding import Mesh
from jax.sharding import PartitionSpec as P

D = 4096
FF = 6144
BLOCK = 128
STEP = 10
LANES = 128
LIVE = 3
AXES = ("y", "z", "core", "z_lo", "x")
DP = ("y", "z", "core")
MP = ("z_lo", "x")
SIZES = {"y": 4, "z": 4, "core": 2, "z_lo": 2, "x": 4}

PAIRS = (
    (256, ((("y", 1), ("y", 3), ("z", 1), ("z", 3)), (("y", 3), ("y", 1), ("z", 3), ("z", 1)))),
    (128, ((("z", 1), ("z", 3), ("y", 1), ("y", 3)), (("z", 3), ("z", 1), ("y", 3), ("y", 1)))),
)
STREAMS = 2 * len(PAIRS)
FLAT = [sum(16 * rows for rows, _ in PAIRS[:n]) for n in range(len(PAIRS) + 1)]
ORDER = (
    "sent:00", "sent:01", "sent:10", "sent:11", "rest",
    "first:00", "start:00", "first:01", "start:01", "first:10", "start:10", "first:11", "start:11",
    "kept", "keep:00", "keep:01", "keep:10", "keep:11",
    "end:00", "start:00", "end:01", "start:01", "end:10", "start:10", "end:11", "start:11",
    "end:00", "start:00", "end:01", "start:01", "end:10", "start:10", "end:11", "start:11",
    "end:10", "start:10", "end:11", "start:11", "end:00", "start:00", "end:01", "start:01",
    "end:10", "end:11", "end:00", "end:01",
)


def swap(value, axis, mask):
    return lax.ppermute(value, axis, [(i, i ^ mask) for i in range(SIZES[axis])])


def place_of_tile(step, t, core):
    y_off = (1 - step // 2) * 1 ^ (1 - step % 2) * 3
    z_off = (1 - t // 2) * 1 ^ (1 - t % 2) * 3
    y, z = lax.axis_index("y") ^ y_off, lax.axis_index("z") ^ z_off
    return (y * 4 + z) * 2 + core


def multiply(mt_ref, x_buf, stores, ready=lambda i: None):
    for i in range(4):
        ready(i)
        runs, first = [], 0
        for n, (rows, kinds) in enumerate(PAIRS):
            for half, steps in enumerate(kinds):
                tiles = []
                for t in range(4):
                    bit = {("y", 1): i // 2, ("y", 3): i % 2, ("z", 1): t // 2, ("z", 3): t % 2}
                    at = [bit[step] for step in steps]
                    if stores[at[0]]:
                        tiles.append((t, at[0], 4 * at[1] + 2 * at[2] + at[3]))
                lanes = [t for t, _, _ in tiles]
                if runs and runs[-1][0] == lanes:
                    runs[-1][1].append((n, half, first, tiles))
                else:
                    runs.append((lanes, [(n, half, first, tiles)]))
                first += rows
        for lanes, members in runs:
            if not lanes:
                continue
            low, high = members[0][2], members[-1][2] + PAIRS[members[-1][0]][0]
            pieces = [x_buf[i, :, :, t * LANES : (t + 1) * LANES] for t in lanes]
            right = x_buf[i] if len(lanes) == 4 else jnp.concatenate(pieces, axis=2)
            total = jnp.dot(
                mt_ref[low:high],
                right.reshape(LIVE * 256, len(lanes) * LANES),
                preferred_element_type=jnp.float32,
            )
            for n, half, first, tiles in members:
                rows = slice(first - low, first - low + PAIRS[n][0])
                for k, (_, kept, place) in enumerate(tiles):
                    stores[kept](n, half, place, total[rows, k * LANES : (k + 1) * LANES])


def into(refs):
    def store(n, half, place, value):
        refs[2 * n + half][place // 4, place // 2 % 2, place % 2] = value

    return store


def into_flat(ref):
    def store(n, half, place, value):
        rows = PAIRS[n][0]
        first = FLAT[n] + (8 * half + place) * rows
        ref[first : first + rows] = value

    return store


def load_numbers(ff_hbm, active_hbm, ff_ref, active_ref, sem):
    copies = [
        pltpu.make_async_copy(ff_hbm, ff_ref, sem.at[0]),
        pltpu.make_async_copy(active_hbm, active_ref, sem.at[1]),
    ]
    for c in copies:
        c.start()
    for c in copies:
        c.wait()
    idle = sum(jnp.where(active_ref[i] == 1, 0, i) for i in range(1, 4))
    return [s + (s >= idle).astype(jnp.int32) for s in range(LIVE)]


def load_tiles(x_ref, x_buf, x_sem, live, core):
    for i in range(4):
        for t in range(4):
            column = pl.multiple_of(place_of_tile(i, t, core) * LANES, LANES)
            for s in range(LIVE):
                pltpu.make_async_copy(
                    x_ref.at[live[s], :, pl.ds(column, LANES)],
                    x_buf.at[i, s, :, pl.ds(t * LANES, LANES)],
                    x_sem.at[i],
                ).start()

    def ready(i):
        pltpu.make_async_copy(x_buf.at[i], x_buf.at[i], x_sem.at[i]).wait()

    return ready


def sent_kernel(ff_hbm, active_hbm, x_ref, m_ref, *refs):
    outs, refs = refs[:STREAMS], refs[STREAMS:]
    x_buf, mt_ref, ff_ref, active_ref, sem, x_sem, m_buf, m_sem = refs
    live = load_numbers(ff_hbm, active_hbm, ff_ref, active_ref, sem)
    for s in range(LIVE):
        pltpu.make_async_copy(m_ref.at[live[s]], m_buf.at[s], m_sem).start()
    ready = load_tiles(x_ref, x_buf, x_sem, live, 1 - lax.axis_index("core"))
    pltpu.make_async_copy(m_buf, m_buf, m_sem).wait()
    cols = m_buf.shape[2]
    first = lax.axis_index(MP) * cols
    for s in range(LIVE):
        values = m_buf[s]
        column = first + lax.broadcasted_iota(jnp.int32, values.shape, 1)
        keep = column < BLOCK * ff_ref[live[s]]
        values = jnp.where(keep, values, jnp.zeros_like(values))
        mt_ref[:, s * 256 : (s + 1) * 256] = values.T
    multiply(mt_ref, x_buf, (into(outs), None), ready)


def rest_kernel(ff_hbm, active_hbm, x_ref, mt_ref, other_x, *refs):
    other_kept, refs = refs[0], refs[1:]
    sent, kept = refs[:STREAMS], refs[STREAMS : 2 * STREAMS]
    ff_ref, active_ref, sem, x_buf, x_sem = refs[2 * STREAMS :]
    live = load_numbers(ff_hbm, active_hbm, ff_ref, active_ref, sem)
    ready = load_tiles(x_ref, x_buf, x_sem, live, lax.axis_index("core"))
    multiply(mt_ref, other_x, (None, into_flat(other_kept)))
    multiply(mt_ref, x_buf, (into(sent), into(kept)), ready)


def call(kernel, operands, spaces, out_shape, scratch, mebibytes):
    return pl.pallas_call(
        kernel,
        in_specs=[pl.BlockSpec(memory_space=space) for space in spaces],
        out_specs=[pl.BlockSpec(memory_space=pltpu.VMEM)] * len(out_shape),
        scratch_shapes=[
            pltpu.SMEM((4,), jnp.int32),
            pltpu.SMEM((4,), jnp.int32),
            pltpu.SemaphoreType.DMA((2,)),
            *scratch,
        ],
        out_shape=out_shape,
        compiler_params=pltpu.CompilerParams(vmem_limit_bytes=mebibytes * 1024 * 1024),
    )(*(pltpu.with_memory_space_constraint(o, s) for o, s in zip(operands, spaces)))


def products(ff_blocks, layer_active, x, m):
    hbm, vmem = pltpu.HBM, pltpu.VMEM
    pieces = [vmem((2, 2, 2, rows, LANES), jnp.float32) for rows, _ in PAIRS for _ in range(2)]
    tiles = vmem((4, LIVE, 256, 4 * LANES), jnp.bfloat16)
    sems = pltpu.SemaphoreType.DMA((4,))
    turned = vmem((m.shape[2], LIVE * 256), jnp.bfloat16)
    *sent, other_x, turned = call(
        sent_kernel,
        (ff_blocks, layer_active, x, m),
        (hbm, hbm, hbm, hbm),
        pieces + [tiles, turned],
        [sems, vmem((LIVE, 256, m.shape[2]), jnp.bfloat16), pltpu.SemaphoreType.DMA],
        6,
    )

    def rest(tie):
        return call(
            rest_kernel,
            (ff_blocks, layer_active, x, tie(turned), other_x),
            (hbm, hbm, hbm, vmem, vmem),
            [vmem((FLAT[-1], LANES), jnp.float32)] + pieces + pieces,
            [tiles, sems],
            8,
        )

    return sent, rest


class Stream:
    def __init__(self, steps):
        self.steps, self.at = steps, 0
        self.send = self.keep = self.flying = None


class Line:
    def __init__(self, token):
        self.token = token

    def tie(self, *values):
        *values, self.token = lax.optimization_barrier((*values, self.token))
        return values[0] if len(values) == 1 else values

    def first(self, stream, own, other):
        stream.send = self.token = self.tie(own + other)

    def keep(self, stream, own, other):
        stream.keep = self.token = self.tie(own + other)
        stream.keep = [stream.keep]

    def start(self, stream):
        axis, mask = stream.steps[stream.at]
        self.token = send = self.tie(stream.send)
        stream.flying = swap(send, axis, mask)
        stream.at += 1

    def end(self, stream):
        parts = stream.keep + [self.tie(stream.flying)]
        if stream.at < len(stream.steps):
            stream.send = self.token = self.tie(sum(p[0] for p in parts[1:]) + parts[0][0])
            stream.keep = [p[1] for p in parts]
        else:
            stream.send = self.token = self.tie(sum(parts[1:]) + parts[0])


def shards(inputs, gate_cotangent, ff_blocks, layer_active, param, moment, second_moment):
    sent, rest = products(ff_blocks, layer_active, inputs, gate_cotangent)
    flying, line = {}, Line(sent[0])
    streams = {(n, half): Stream(pair[1][half]) for n, pair in enumerate(PAIRS) for half in range(2)}
    for act, *names in (event.split(":") for event in ORDER):
        if act == "rest":
            other_kept, *owns = rest(line.tie)
            line.token = owns[0]
            continue
        if act == "kept":
            line.token = line.tie(other_kept)
            flat = line.tie(swap(line.token, "core", 1))
            continue
        n, half = (int(c) for c in names[0])
        if act == "sent":
            line.token = line.tie(sent[2 * n + half])
            flying[n, half] = swap(line.token, "core", 1)
        elif act == "first":
            line.first(streams[n, half], owns[2 * n + half], line.tie(flying[n, half]))
        elif act == "keep":
            own = owns[STREAMS + 2 * n + half]
            first = FLAT[n] + half * own.size // LANES
            other = flat[first : first + own.size // LANES].reshape(own.shape)
            line.keep(streams[n, half], own, other)
        else:
            getattr(line, act)(streams[n, half])
    done = [stream.send for stream in streams.values()]
    squares = sum(jnp.sum(t * t, axis=0, keepdims=True) for t in done)
    devices = math.prod(SIZES[a] for a in DP)
    squares = lax.all_to_all(jnp.broadcast_to(squares[None], (devices, 1, LANES)), DP, 0, 0, tiled=True)
    squares = jnp.sum(squares, axis=0)
    blocks = jnp.concatenate(done, axis=0).T.reshape(8, -1, gate_cotangent.shape[2])
    beside = jnp.broadcast_to(squares[None], blocks.shape[:2] + (LANES,))
    blocks = lax.all_to_all(jnp.concatenate([blocks, beside], axis=2), MP, 0, 0, tiled=True)
    total = jnp.sqrt(jnp.sum(blocks[:, 0, -LANES:]))
    gradient = blocks[:, :, :-LANES].transpose(1, 0, 2).reshape(param.shape)
    factor = jnp.minimum(1.0, math.sqrt(1.0 * D * FF) / (total + 1e-06))
    clipped = gradient * factor
    new_moment = 0.9 * moment + 0.1 * clipped
    new_second = 0.95 * second_moment + 0.05 * clipped * clipped
    first_hat = new_moment / (1.0 - 0.9**STEP)
    second_hat = new_second / (1.0 - 0.95**STEP)
    new_param = param - 0.02 * (first_hat / (jnp.sqrt(second_hat) + 1e-08) + 0.1 * param)
    return (new_param, new_moment, new_second)


def solution(mesh):
    split = Mesh(mesh.devices.reshape(4, 4, 2, 2, 4), AXES)
    rows = P(AXES, None)
    return jax.shard_map(
        shards,
        mesh=split,
        in_specs=(P(None, DP, None), P(None, DP, MP), P(), P(), rows, rows, rows),
        out_specs=(rows, rows, rows),
        check_vma=False,
    )
```

```python
import functools
import math

import jax
import jax.numpy as jnp
from jax import lax
from jax.experimental import pallas as pl
from jax.experimental.pallas import tpu as pltpu
from jax.sharding import Mesh
from jax.sharding import PartitionSpec as P

D = 4096
FF = 6144
BLOCK = 128
STEP = 10
LANES = 128
LIVE = 3
AXES = ("y", "z", "core", "z_lo", "x")
DP = ("y", "z", "core")
MP = ("z_lo", "x")
SIZES = {"y": 4, "z": 4, "core": 2, "z_lo": 2, "x": 4}

PAIRS = (
    (256, ((("y", 1), ("y", 3), ("z", 1), ("z", 3)), (("y", 3), ("y", 1), ("z", 3), ("z", 1)))),
    (128, ((("z", 1), ("z", 3), ("y", 1), ("y", 3)), (("z", 3), ("z", 1), ("y", 3), ("y", 1)))),
)
STREAMS = 2 * len(PAIRS)
FLAT = [sum(16 * rows for rows, _ in PAIRS[:n]) for n in range(len(PAIRS) + 1)]
ORDER = (
    "sent:00", "sent:01", "sent:10", "sent:11", "rest",
    "first:00", "first:01", "first:10", "first:11", "start:00", "start:01", "start:10", "start:11",
    "kept", "keep:00", "keep:01", "end:00", "end:01", "start:00", "start:01",
    "keep:10", "keep:11", "end:10", "start:10", "end:11", "start:11",
    "end:00", "start:00", "end:01", "start:01", "end:10", "start:10", "end:11", "start:11",
    "end:10", "start:10", "end:11", "start:11", "end:00", "start:00", "end:01", "start:01",
    "end:10", "end:11", "end:00", "end:01",
)


def swap(value, axis, mask):
    return lax.ppermute(value, axis, [(i, i ^ mask) for i in range(SIZES[axis])])


def place_of_tile(step, t, core):
    y_off = (1 - step // 2) * 1 ^ (1 - step % 2) * 3
    z_off = (1 - t // 2) * 1 ^ (1 - t % 2) * 3
    y, z = lax.axis_index("y") ^ y_off, lax.axis_index("z") ^ z_off
    return (y * 4 + z) * 2 + core


def multiply(mt_ref, x_buf, stores, ready=lambda i: None):
    for i in range(4):
        ready(i)
        runs, first = [], 0
        for n, (rows, kinds) in enumerate(PAIRS):
            for half, steps in enumerate(kinds):
                tiles = []
                for t in range(4):
                    bit = {("y", 1): i // 2, ("y", 3): i % 2, ("z", 1): t // 2, ("z", 3): t % 2}
                    at = [bit[step] for step in steps]
                    if stores[at[0]]:
                        tiles.append((t, at[0], 4 * at[1] + 2 * at[2] + at[3]))
                lanes = [t for t, _, _ in tiles]
                if runs and runs[-1][0] == lanes:
                    runs[-1][1].append((n, half, first, tiles))
                else:
                    runs.append((lanes, [(n, half, first, tiles)]))
                first += rows
        for lanes, members in runs:
            if not lanes:
                continue
            low, high = members[0][2], members[-1][2] + PAIRS[members[-1][0]][0]
            pieces = [x_buf[i, :, :, t * LANES : (t + 1) * LANES] for t in lanes]
            right = x_buf[i] if len(lanes) == 4 else jnp.concatenate(pieces, axis=2)
            total = jnp.dot(
                mt_ref[low:high],
                right.reshape(LIVE * 256, len(lanes) * LANES),
                preferred_element_type=jnp.float32,
            )
            for n, half, first, tiles in members:
                rows = slice(first - low, first - low + PAIRS[n][0])
                for k, (_, kept, place) in enumerate(tiles):
                    stores[kept](n, half, place, total[rows, k * LANES : (k + 1) * LANES])


def into(refs):
    def store(n, half, place, value):
        refs[2 * n + half][place // 4, place // 2 % 2, place % 2] = value

    return store


def into_flat(ref):
    def store(n, half, place, value):
        rows = PAIRS[n][0]
        first = FLAT[n] + (8 * half + place) * rows
        ref[first : first + rows] = value

    return store


def load_tiles(x_ref, x_buf, x_sem, subnet, s, core):
    for i in range(4):
        for t in range(4):
            column = pl.multiple_of(place_of_tile(i, t, core) * LANES, LANES)
            pltpu.make_async_copy(
                x_ref.at[subnet, :, pl.ds(column, LANES)],
                x_buf.at[i, s, :, pl.ds(t * LANES, LANES)],
                x_sem.at[i],
            ).start()


def await_tiles(x_buf, x_sem, i):
    pltpu.make_async_copy(x_buf.at[i], x_buf.at[i], x_sem.at[i]).wait()


def sent_kernel(ff_hbm, active_hbm, x_ref, m_ref, *refs):
    outs, refs = refs[:STREAMS], refs[STREAMS:]
    x_other, x_own, mt_ref, ff_ref, active_ref, sem, x_sem, own_sem, m_buf, m_sem = refs
    numbers = [
        pltpu.make_async_copy(ff_hbm, ff_ref, sem.at[0]),
        pltpu.make_async_copy(active_hbm, active_ref, sem.at[1]),
    ]
    all_m = pltpu.make_async_copy(m_ref, m_buf, m_sem)
    for c in (*numbers, all_m):
        c.start()
    core = lax.axis_index("core")
    load_tiles(x_ref, x_other, x_sem, 0, 0, 1 - core)
    for c in numbers:
        c.wait()
    idle = sum(jnp.where(active_ref[i] == 1, 0, i) for i in range(1, 4))
    live = [s + (s >= idle).astype(jnp.int32) for s in range(LIVE)]
    for s in range(1, LIVE):
        load_tiles(x_ref, x_other, x_sem, live[s], s, 1 - core)
    for s in range(LIVE):
        load_tiles(x_ref, x_own, own_sem, live[s], s, core)
    all_m.wait()
    cols = m_buf.shape[2]
    first = lax.axis_index(MP) * cols
    for s in range(LIVE):
        values = m_buf[live[s]]
        column = first + lax.broadcasted_iota(jnp.int32, values.shape, 1)
        keep = column < BLOCK * ff_ref[live[s]]
        values = jnp.where(keep, values, jnp.zeros_like(values))
        mt_ref[:, s * 256 : (s + 1) * 256] = values.T
    multiply(mt_ref, x_other, (into(outs), None), functools.partial(await_tiles, x_other, x_sem))
    for i in range(4):
        await_tiles(x_own, own_sem, i)


def rest_kernel(mt_ref, x_other, x_own, other_kept, *refs):
    sent, kept = refs[:STREAMS], refs[STREAMS:]
    multiply(mt_ref, x_other, (None, into_flat(other_kept)))
    multiply(mt_ref, x_own, (into(sent), into(kept)))


def call(kernel, operands, spaces, out_shape, scratch, mebibytes):
    return pl.pallas_call(
        kernel,
        in_specs=[pl.BlockSpec(memory_space=space) for space in spaces],
        out_specs=[pl.BlockSpec(memory_space=pltpu.VMEM)] * len(out_shape),
        scratch_shapes=scratch,
        out_shape=out_shape,
        compiler_params=pltpu.CompilerParams(vmem_limit_bytes=mebibytes * 1024 * 1024),
    )(*(pltpu.with_memory_space_constraint(o, s) for o, s in zip(operands, spaces)))


def products(ff_blocks, layer_active, x, m):
    hbm, vmem, sems = pltpu.HBM, pltpu.VMEM, pltpu.SemaphoreType.DMA
    pieces = [vmem((2, 2, 2, rows, LANES), jnp.float32) for rows, _ in PAIRS for _ in range(2)]
    tiles = vmem((4, LIVE, 256, 4 * LANES), jnp.bfloat16)
    *sent, x_other, x_own, turned = call(
        sent_kernel,
        (ff_blocks, layer_active, x, m),
        (hbm, hbm, hbm, hbm),
        pieces + [tiles, tiles, vmem((m.shape[2], LIVE * 256), jnp.bfloat16)],
        [
            pltpu.SMEM((4,), jnp.int32),
            pltpu.SMEM((4,), jnp.int32),
            sems((2,)),
            sems((4,)),
            sems((4,)),
            vmem(m.shape, jnp.bfloat16),
            sems,
        ],
        6,
    )

    def rest(tie):
        return call(
            rest_kernel,
            (tie(turned), x_other, x_own),
            (vmem, vmem, vmem),
            [vmem((FLAT[-1], LANES), jnp.float32)] + pieces + pieces,
            [],
            6,
        )

    return sent, rest


def sum_kernel(*refs):
    for own, other, out in zip(refs[:STREAMS], refs[STREAMS : 2 * STREAMS], refs[2 * STREAMS :]):
        def step(k, _):
            at = k // 4, k // 2 % 2, k % 2
            out[at] = own[at] + other[at]
            return 0

        lax.fori_loop(0, 8, step, 0)


def sums(owns, others):
    return pl.pallas_call(
        sum_kernel,
        in_specs=[pl.BlockSpec(memory_space=pltpu.VMEM)] * (2 * STREAMS),
        out_specs=[pl.BlockSpec(memory_space=pltpu.VMEM)] * STREAMS,
        out_shape=[pltpu.VMEM(o.shape, o.dtype) for o in owns],
        input_output_aliases={n: n for n in range(STREAMS)},
        compiler_params=pltpu.CompilerParams(vmem_limit_bytes=2 * 1024 * 1024),
    )(*(pltpu.with_memory_space_constraint(o, pltpu.VMEM) for o in (*owns, *others)))


class Stream:
    def __init__(self, steps):
        self.steps, self.at = steps, 0
        self.send = self.keep = self.flying = None


class Line:
    def __init__(self, token):
        self.token = token

    def tie(self, *values):
        *values, self.token = lax.optimization_barrier((*values, self.token))
        return values[0] if len(values) == 1 else values

    def keep(self, stream, own, other):
        stream.keep = self.token = self.tie(own + other)
        stream.keep = [stream.keep]

    def start(self, stream):
        axis, mask = stream.steps[stream.at]
        self.token = send = self.tie(stream.send)
        stream.flying = swap(send, axis, mask)
        stream.at += 1

    def end(self, stream):
        parts = stream.keep + [self.tie(stream.flying)]
        if stream.at < len(stream.steps):
            stream.send = self.token = self.tie(sum(p[0] for p in parts[1:]) + parts[0][0])
            stream.keep = [p[1] for p in parts]
        else:
            stream.send = self.token = self.tie(sum(parts[1:]) + parts[0])


def shards(inputs, gate_cotangent, ff_blocks, layer_active, param, moment, second_moment):
    sent, rest = products(ff_blocks, layer_active, inputs, gate_cotangent)
    flying, firsts, line = {}, None, Line(sent[0])
    streams = {(n, half): Stream(pair[1][half]) for n, pair in enumerate(PAIRS) for half in range(2)}
    for act, *names in (event.split(":") for event in ORDER):
        if act == "rest":
            other_kept, *owns = rest(line.tie)
            line.token = owns[0]
            continue
        if act == "kept":
            line.token = line.tie(other_kept)
            flat = line.tie(swap(line.token, "core", 1))
            continue
        n, half = (int(c) for c in names[0])
        if act == "sent":
            line.token = line.tie(sent[2 * n + half])
            flying[n, half] = swap(line.token, "core", 1)
        elif act == "first":
            if not firsts:
                others = [line.tie(f) for f in flying.values()]
                firsts = sums(owns[:STREAMS], others)
                line.token = firsts[0]
            streams[n, half].send = firsts[2 * n + half]
        elif act == "keep":
            own = owns[STREAMS + 2 * n + half]
            first = FLAT[n] + half * own.size // LANES
            other = flat[first : first + own.size // LANES].reshape(own.shape)
            line.keep(streams[n, half], own, other)
        else:
            getattr(line, act)(streams[n, half])
    done = [stream.send for stream in streams.values()]
    squares = sum(jnp.sum(t * t, axis=0, keepdims=True) for t in done)
    devices = math.prod(SIZES[a] for a in DP)
    squares = lax.all_to_all(jnp.broadcast_to(squares[None], (devices, 1, LANES)), DP, 0, 0, tiled=True)
    squares = jnp.sum(squares, axis=0)
    blocks = jnp.concatenate(done, axis=0).T.reshape(8, -1, gate_cotangent.shape[2])
    beside = jnp.broadcast_to(squares[None], blocks.shape[:2] + (LANES,))
    blocks = lax.all_to_all(jnp.concatenate([blocks, beside], axis=2), MP, 0, 0, tiled=True)
    total = jnp.sqrt(jnp.sum(blocks[:, 0, -LANES:]))
    gradient = blocks[:, :, :-LANES].transpose(1, 0, 2).reshape(param.shape)
    factor = jnp.minimum(1.0, math.sqrt(1.0 * D * FF) / (total + 1e-06))
    clipped = gradient * factor
    new_moment = 0.9 * moment + 0.1 * clipped
    new_second = 0.95 * second_moment + 0.05 * clipped * clipped
    first_hat = new_moment / (1.0 - 0.9**STEP)
    second_hat = new_second / (1.0 - 0.95**STEP)
    new_param = param - 0.02 * (first_hat / (jnp.sqrt(second_hat) + 1e-08) + 0.1 * param)
    return (new_param, new_moment, new_second)


def solution(mesh):
    split = Mesh(mesh.devices.reshape(4, 4, 2, 2, 4), AXES)
    rows = P(AXES, None)
    return jax.shard_map(
        shards,
        mesh=split,
        in_specs=(P(None, DP, None), P(None, DP, MP), P(), P(), rows, rows, rows),
        out_specs=(rows, rows, rows),
        check_vma=False,
    )
```

```python
import functools
import math

import jax
import jax.numpy as jnp
from jax import lax
from jax.experimental import pallas as pl
from jax.experimental.pallas import tpu as pltpu
from jax.sharding import Mesh
from jax.sharding import PartitionSpec as P

D = 4096
FF = 6144
BLOCK = 128
STEP = 10
LANES = 128
LIVE = 3
AXES = ("y", "z", "core", "z_lo", "x")
DP = ("y", "z", "core")
MP = ("z_lo", "x")
SIZES = {"y": 4, "z": 4, "core": 2, "z_lo": 2, "x": 4}

PAIRS = (
    (256, ((("y", 1), ("y", 3), ("z", 1), ("z", 3)), (("y", 3), ("y", 1), ("z", 3), ("z", 1)))),
    (128, ((("z", 1), ("z", 3), ("y", 1), ("y", 3)), (("z", 3), ("z", 1), ("y", 3), ("y", 1)))),
)
STREAMS = 2 * len(PAIRS)
FLAT = [sum(16 * rows for rows, _ in PAIRS[:n]) for n in range(len(PAIRS) + 1)]
ORDER = (
    "sent:0", "sent:1", "rest",
    "first:00", "first:01", "first:10", "first:11", "start:00", "start:01", "start:10", "start:11",
    "kept", "keep:00", "keep:01", "end:00", "end:01", "start:00", "start:01",
    "keep:10", "keep:11", "end:10", "start:10", "end:11", "start:11",
    "end:00", "start:00", "end:01", "start:01", "end:10", "start:10", "end:11", "start:11",
    "end:10", "start:10", "end:11", "start:11", "end:00", "start:00", "end:01", "start:01",
    "end:10", "end:11", "end:00", "end:01",
)


def swap(value, axis, mask):
    return lax.ppermute(value, axis, [(i, i ^ mask) for i in range(SIZES[axis])])


def place_of_tile(step, t, core):
    y_off = (1 - step // 2) * 1 ^ (1 - step % 2) * 3
    z_off = (1 - t // 2) * 1 ^ (1 - t % 2) * 3
    y, z = lax.axis_index("y") ^ y_off, lax.axis_index("z") ^ z_off
    return (y * 4 + z) * 2 + core


def multiply(mt_ref, x_buf, stores, ready=lambda i: None):
    for i in range(4):
        ready(i)
        runs, first = [], 0
        for n, (rows, kinds) in enumerate(PAIRS):
            for half, steps in enumerate(kinds):
                tiles = []
                for t in range(4):
                    bit = {("y", 1): i // 2, ("y", 3): i % 2, ("z", 1): t // 2, ("z", 3): t % 2}
                    at = [bit[step] for step in steps]
                    if stores[at[0]]:
                        tiles.append((t, at[0], 4 * at[1] + 2 * at[2] + at[3]))
                lanes = [t for t, _, _ in tiles]
                if runs and runs[-1][0] == lanes:
                    runs[-1][1].append((n, half, first, tiles))
                else:
                    runs.append((lanes, [(n, half, first, tiles)]))
                first += rows
        for lanes, members in runs:
            if not lanes:
                continue
            low, high = members[0][2], members[-1][2] + PAIRS[members[-1][0]][0]
            pieces = [x_buf[i, :, :, t * LANES : (t + 1) * LANES] for t in lanes]
            right = x_buf[i] if len(lanes) == 4 else jnp.concatenate(pieces, axis=2)
            total = jnp.dot(
                mt_ref[low:high],
                right.reshape(LIVE * 256, len(lanes) * LANES),
                preferred_element_type=jnp.float32,
            )
            for n, half, first, tiles in members:
                rows = slice(first - low, first - low + PAIRS[n][0])
                for k, (_, kept, place) in enumerate(tiles):
                    stores[kept](n, half, place, total[rows, k * LANES : (k + 1) * LANES])


def into(refs):
    def store(n, half, place, value):
        refs[2 * n + half][place // 4, place // 2 % 2, place % 2] = value

    return store


def into_pairs(refs):
    def store(n, half, place, value):
        refs[n][half, place // 4, place // 2 % 2, place % 2] = value

    return store


def into_flat(ref):
    def store(n, half, place, value):
        rows = PAIRS[n][0]
        first = FLAT[n] + (8 * half + place) * rows
        ref[first : first + rows] = value

    return store


def load_tiles(x_ref, x_buf, x_sem, subnet, s, core):
    for i in range(4):
        for t in range(4):
            column = pl.multiple_of(place_of_tile(i, t, core) * LANES, LANES)
            pltpu.make_async_copy(
                x_ref.at[subnet, :, pl.ds(column, LANES)],
                x_buf.at[i, s, :, pl.ds(t * LANES, LANES)],
                x_sem.at[i],
            ).start()


def await_tiles(x_buf, x_sem, i):
    pltpu.make_async_copy(x_buf.at[i], x_buf.at[i], x_sem.at[i]).wait()


def sent_kernel(ff_hbm, active_hbm, x_ref, m_ref, *refs):
    outs, refs = refs[: len(PAIRS)], refs[len(PAIRS) :]
    x_other, x_own, mt_ref, ff_ref, active_ref, sem, x_sem, own_sem, m_buf, m_sem = refs
    numbers = [
        pltpu.make_async_copy(ff_hbm, ff_ref, sem.at[0]),
        pltpu.make_async_copy(active_hbm, active_ref, sem.at[1]),
    ]
    all_m = pltpu.make_async_copy(m_ref, m_buf, m_sem)
    for c in (*numbers, all_m):
        c.start()
    core = lax.axis_index("core")
    load_tiles(x_ref, x_other, x_sem, 0, 0, 1 - core)
    for c in numbers:
        c.wait()
    idle = sum(jnp.where(active_ref[i] == 1, 0, i) for i in range(1, 4))
    live = [s + (s >= idle).astype(jnp.int32) for s in range(LIVE)]
    for s in range(1, LIVE):
        load_tiles(x_ref, x_other, x_sem, live[s], s, 1 - core)
    for s in range(LIVE):
        load_tiles(x_ref, x_own, own_sem, live[s], s, core)
    all_m.wait()
    cols = m_buf.shape[2]
    first = lax.axis_index(MP) * cols
    for s in range(LIVE):
        values = m_buf[live[s]]
        column = first + lax.broadcasted_iota(jnp.int32, values.shape, 1)
        keep = column < BLOCK * ff_ref[live[s]]
        values = jnp.where(keep, values, jnp.zeros_like(values))
        mt_ref[:, s * 256 : (s + 1) * 256] = values.T
    multiply(mt_ref, x_other, (into_pairs(outs), None), functools.partial(await_tiles, x_other, x_sem))
    for i in range(4):
        await_tiles(x_own, own_sem, i)


def rest_kernel(mt_ref, x_other, x_own, other_kept, *refs):
    sent, kept = refs[:STREAMS], refs[STREAMS:]
    multiply(mt_ref, x_other, (None, into_flat(other_kept)))
    multiply(mt_ref, x_own, (into(sent), into(kept)))


def call(kernel, operands, spaces, out_shape, scratch, mebibytes):
    return pl.pallas_call(
        kernel,
        in_specs=[pl.BlockSpec(memory_space=space) for space in spaces],
        out_specs=[pl.BlockSpec(memory_space=pltpu.VMEM)] * len(out_shape),
        scratch_shapes=scratch,
        out_shape=out_shape,
        compiler_params=pltpu.CompilerParams(vmem_limit_bytes=mebibytes * 1024 * 1024),
    )(*(pltpu.with_memory_space_constraint(o, s) for o, s in zip(operands, spaces)))


def products(ff_blocks, layer_active, x, m):
    hbm, vmem, sems = pltpu.HBM, pltpu.VMEM, pltpu.SemaphoreType.DMA
    pieces = [vmem((2, 2, 2, rows, LANES), jnp.float32) for rows, _ in PAIRS for _ in range(2)]
    tiles = vmem((4, LIVE, 256, 4 * LANES), jnp.bfloat16)
    *sent, x_other, x_own, turned = call(
        sent_kernel,
        (ff_blocks, layer_active, x, m),
        (hbm, hbm, hbm, hbm),
        [vmem((2, 2, 2, 2, rows, LANES), jnp.float32) for rows, _ in PAIRS] + [tiles, tiles, vmem((m.shape[2], LIVE * 256), jnp.bfloat16)],
        [
            pltpu.SMEM((4,), jnp.int32),
            pltpu.SMEM((4,), jnp.int32),
            sems((2,)),
            sems((4,)),
            sems((4,)),
            vmem(m.shape, jnp.bfloat16),
            sems,
        ],
        6,
    )

    def rest(tie):
        return call(
            rest_kernel,
            (tie(turned), x_other, x_own),
            (vmem, vmem, vmem),
            [vmem((FLAT[-1], LANES), jnp.float32)] + pieces + pieces,
            [],
            6,
        )

    return sent, rest


def sum_kernel(*refs):
    owns, others, outs = refs[:STREAMS], refs[STREAMS:-STREAMS], refs[-STREAMS:]
    for n, (own, out) in enumerate(zip(owns, outs)):
        def step(k, _):
            at = k // 4, k // 2 % 2, k % 2
            out[at] = own[at] + others[n // 2][(n % 2, *at)]
            return 0

        lax.fori_loop(0, 8, step, 0)


def sums(owns, others):
    return pl.pallas_call(
        sum_kernel,
        in_specs=[pl.BlockSpec(memory_space=pltpu.VMEM)] * (len(owns) + len(others)),
        out_specs=[pl.BlockSpec(memory_space=pltpu.VMEM)] * STREAMS,
        out_shape=[pltpu.VMEM(o.shape, o.dtype) for o in owns],
        input_output_aliases={n: n for n in range(STREAMS)},
        compiler_params=pltpu.CompilerParams(vmem_limit_bytes=2 * 1024 * 1024),
    )(*(pltpu.with_memory_space_constraint(o, pltpu.VMEM) for o in (*owns, *others)))


class Stream:
    def __init__(self, steps):
        self.steps, self.at = steps, 0
        self.send = self.keep = self.flying = None


class Line:
    def __init__(self, token):
        self.token = token

    def tie(self, *values):
        *values, self.token = lax.optimization_barrier((*values, self.token))
        return values[0] if len(values) == 1 else values

    def keep(self, stream, own, other):
        stream.keep = self.token = self.tie(own + other)
        stream.keep = [stream.keep]

    def start(self, stream):
        axis, mask = stream.steps[stream.at]
        self.token = send = self.tie(stream.send)
        stream.flying = swap(send, axis, mask)
        stream.at += 1

    def end(self, stream):
        parts = stream.keep + [self.tie(stream.flying)]
        if stream.at < len(stream.steps):
            stream.send = self.token = self.tie(sum(p[0] for p in parts[1:]) + parts[0][0])
            stream.keep = [p[1] for p in parts]
        else:
            stream.send = self.token = self.tie(sum(parts[1:]) + parts[0])


def message_kernel(*refs):
    *parts, out = refs
    total = sum(jnp.sum((p[...] * p[...]).reshape(-1, 8, LANES), axis=0) for p in parts)
    total = jnp.sum(jnp.sum(total, axis=0, keepdims=True), axis=1, keepdims=True)
    out[...] = jnp.broadcast_to(total[None], out.shape)


def message(parts):
    devices = math.prod(SIZES[a] for a in DP)
    return pl.pallas_call(
        message_kernel,
        in_specs=[pl.BlockSpec(memory_space=pltpu.VMEM)] * len(parts),
        out_specs=pl.BlockSpec(memory_space=pltpu.VMEM),
        out_shape=jax.ShapeDtypeStruct((devices, 1, LANES), jnp.float32),
        compiler_params=pltpu.CompilerParams(vmem_limit_bytes=2 * 1024 * 1024),
    )(*parts)


def shards(inputs, gate_cotangent, ff_blocks, layer_active, param, moment, second_moment):
    sent, rest = products(ff_blocks, layer_active, inputs, gate_cotangent)
    flying, firsts, line = {}, None, Line(sent[0])
    streams = {(n, half): Stream(pair[1][half]) for n, pair in enumerate(PAIRS) for half in range(2)}
    for act, *names in (event.split(":") for event in ORDER):
        if act == "rest":
            other_kept, *owns = rest(line.tie)
            line.token = owns[0]
            continue
        if act == "kept":
            line.token = line.tie(other_kept)
            flat = line.tie(swap(line.token, "core", 1))
            continue
        if act == "sent":
            n = int(names[0])
            line.token = line.tie(sent[n])
            flying[n] = swap(line.token, "core", 1)
            continue
        n, half = (int(c) for c in names[0])
        if act == "first":
            if not firsts:
                others = [line.tie(f) for f in flying.values()]
                firsts = sums(owns[:STREAMS], others)
                line.token = firsts[0]
            streams[n, half].send = firsts[2 * n + half]
        elif act == "keep":
            own = owns[STREAMS + 2 * n + half]
            first = FLAT[n] + half * own.size // LANES
            other = flat[first : first + own.size // LANES].reshape(own.shape)
            line.keep(streams[n, half], own, other)
        else:
            getattr(line, act)(streams[n, half])
    done = [stream.send for stream in streams.values()]
    squares = jnp.sum(lax.all_to_all(message(done), DP, 0, 0, tiled=True), axis=0)
    blocks = jnp.concatenate(done, axis=0).T.reshape(8, -1, gate_cotangent.shape[2])
    beside = jnp.broadcast_to(squares[None], blocks.shape[:2] + (LANES,))
    blocks = lax.all_to_all(jnp.concatenate([blocks, beside], axis=2), MP, 0, 0, tiled=True)
    total = jnp.sqrt(jnp.sum(blocks[:, :, -LANES : 1 - LANES], axis=0))
    gradient = blocks[:, :, :-LANES].transpose(1, 0, 2).reshape(param.shape)
    factor = jnp.minimum(1.0, math.sqrt(1.0 * D * FF) / (total + 1e-06))
    clipped = gradient * factor
    new_moment = 0.9 * moment + 0.1 * clipped
    new_second = 0.95 * second_moment + 0.05 * clipped * clipped
    first_hat = new_moment / (1.0 - 0.9**STEP)
    second_hat = new_second / (1.0 - 0.95**STEP)
    new_param = param - 0.02 * (first_hat / (jnp.sqrt(second_hat) + 1e-08) + 0.1 * param)
    return (new_param, new_moment, new_second)


def solution(mesh):
    split = Mesh(mesh.devices.reshape(4, 4, 2, 2, 4), AXES)
    rows = P(AXES, None)
    return jax.shard_map(
        shards,
        mesh=split,
        in_specs=(P(None, DP, None), P(None, DP, MP), P(), P(), rows, rows, rows),
        out_specs=(rows, rows, rows),
        check_vma=False,
    )
```

```python
import functools
import math

import jax
import jax.numpy as jnp
from jax import lax
from jax.experimental import pallas as pl
from jax.experimental.pallas import tpu as pltpu
from jax.sharding import Mesh
from jax.sharding import PartitionSpec as P

D = 4096
FF = 6144
BLOCK = 128
STEP = 10
LANES = 128
LIVE = 3
AXES = ("y", "z", "core", "z_lo", "x")
DP = ("y", "z", "core")
MP = ("z_lo", "x")
SIZES = {"y": 4, "z": 4, "core": 2, "z_lo": 2, "x": 4}

PAIRS = (
    (256, ((("y", 1), ("y", 3), ("z", 1), ("z", 3)), (("y", 3), ("y", 1), ("z", 3), ("z", 1)))),
    (128, ((("z", 1), ("z", 3), ("y", 1), ("y", 3)), (("z", 3), ("z", 1), ("y", 3), ("y", 1)))),
)
STREAMS = 2 * len(PAIRS)
FLAT = [sum(16 * rows for rows, _ in PAIRS[:n]) for n in range(len(PAIRS) + 1)]
ORDER = (
    "sent:0", "sent:1", "rest",
    "first:00", "first:01", "first:10", "first:11", "start:00", "start:01", "start:10", "start:11",
    "kept", "keep:00", "keep:01", "end:00", "end:01", "start:00", "start:01",
    "keep:10", "keep:11", "end:10", "start:10", "end:11", "start:11",
    "end:00", "start:00", "end:01", "start:01", "end:10", "start:10", "end:11", "start:11",
    "end:10", "start:10", "end:11", "start:11", "end:00", "start:00", "end:01", "start:01",
    "end:10", "end:11", "end:00", "end:01",
)


def swap(value, axis, mask):
    return lax.ppermute(value, axis, [(i, i ^ mask) for i in range(SIZES[axis])])


def place_of_tile(step, t, core):
    y_off = (1 - step // 2) * 1 ^ (1 - step % 2) * 3
    z_off = (1 - t // 2) * 1 ^ (1 - t % 2) * 3
    y, z = lax.axis_index("y") ^ y_off, lax.axis_index("z") ^ z_off
    return (y * 4 + z) * 2 + core


def multiply(mt_ref, x_buf, stores, ready=lambda i: None, pairs=(0, 1)):
    for i in range(4):
        ready(i)
        runs, first = [], 0
        for n, (rows, kinds) in enumerate(PAIRS):
            for half, steps in enumerate(kinds):
                tiles = []
                for t in range(4):
                    bit = {("y", 1): i // 2, ("y", 3): i % 2, ("z", 1): t // 2, ("z", 3): t % 2}
                    at = [bit[step] for step in steps]
                    if stores[at[0]] and n in pairs:
                        tiles.append((t, at[0], 4 * at[1] + 2 * at[2] + at[3]))
                lanes = [t for t, _, _ in tiles]
                if runs and runs[-1][0] == lanes:
                    runs[-1][1].append((n, half, first, tiles))
                else:
                    runs.append((lanes, [(n, half, first, tiles)]))
                first += rows
        for lanes, members in runs:
            if not lanes:
                continue
            low, high = members[0][2], members[-1][2] + PAIRS[members[-1][0]][0]
            pieces = [x_buf[i, :, :, t * LANES : (t + 1) * LANES] for t in lanes]
            right = x_buf[i] if len(lanes) == 4 else jnp.concatenate(pieces, axis=2)
            total = jnp.dot(
                mt_ref[low:high],
                right.reshape(LIVE * 256, len(lanes) * LANES),
                preferred_element_type=jnp.float32,
            )
            for n, half, first, tiles in members:
                rows = slice(first - low, first - low + PAIRS[n][0])
                for k, (_, kept, place) in enumerate(tiles):
                    stores[kept](n, half, place, total[rows, k * LANES : (k + 1) * LANES])


def into(refs):
    def store(n, half, place, value):
        refs[2 * n + half][place // 4, place // 2 % 2, place % 2] = value

    return store


def into_pair(ref):
    def store(n, half, place, value):
        ref[half, place // 4, place // 2 % 2, place % 2] = value

    return store


def into_flat(ref):
    def store(n, half, place, value):
        rows = PAIRS[n][0]
        first = FLAT[n] + (8 * half + place) * rows
        ref[first : first + rows] = value

    return store


def load_tiles(x_ref, x_buf, x_sem, subnet, s, core):
    for i in range(4):
        for t in range(4):
            column = pl.multiple_of(place_of_tile(i, t, core) * LANES, LANES)
            pltpu.make_async_copy(
                x_ref.at[subnet, :, pl.ds(column, LANES)],
                x_buf.at[i, s, :, pl.ds(t * LANES, LANES)],
                x_sem.at[i],
            ).start()


def await_tiles(x_buf, x_sem, i):
    pltpu.make_async_copy(x_buf.at[i], x_buf.at[i], x_sem.at[i]).wait()


def sent_kernel(ff_hbm, active_hbm, x_ref, m_ref, *refs):
    out, refs = refs[0], refs[1:]
    x_other, x_own, mt_ref, ff_ref, active_ref, sem, x_sem, own_sem, m_buf, m_sem = refs
    numbers = [
        pltpu.make_async_copy(ff_hbm, ff_ref, sem.at[0]),
        pltpu.make_async_copy(active_hbm, active_ref, sem.at[1]),
    ]
    all_m = pltpu.make_async_copy(m_ref, m_buf, m_sem)
    for c in (*numbers, all_m):
        c.start()
    core = lax.axis_index("core")
    load_tiles(x_ref, x_other, x_sem, 0, 0, 1 - core)
    for c in numbers:
        c.wait()
    idle = sum(jnp.where(active_ref[i] == 1, 0, i) for i in range(1, 4))
    live = [s + (s >= idle).astype(jnp.int32) for s in range(LIVE)]
    for s in range(1, LIVE):
        load_tiles(x_ref, x_other, x_sem, live[s], s, 1 - core)
    for s in range(LIVE):
        load_tiles(x_ref, x_own, own_sem, live[s], s, core)
    all_m.wait()
    cols = m_buf.shape[2]
    first = lax.axis_index(MP) * cols
    for s in range(LIVE):
        values = m_buf[live[s]]
        column = first + lax.broadcasted_iota(jnp.int32, values.shape, 1)
        keep = column < BLOCK * ff_ref[live[s]]
        values = jnp.where(keep, values, jnp.zeros_like(values))
        mt_ref[:, s * 256 : (s + 1) * 256] = values.T
    ready = functools.partial(await_tiles, x_other, x_sem)
    multiply(mt_ref, x_other, (into_pair(out), None), ready, pairs=(0,))
    for i in range(4):
        await_tiles(x_own, own_sem, i)


def next_kernel(mt_ref, x_other, out):
    multiply(mt_ref, x_other, (into_pair(out), None), pairs=(1,))


def rest_kernel(mt_ref, x_other, x_own, other_kept, *refs):
    sent, kept = refs[:STREAMS], refs[STREAMS:]
    multiply(mt_ref, x_other, (None, into_flat(other_kept)))
    multiply(mt_ref, x_own, (into(sent), into(kept)))


def call(kernel, operands, spaces, out_shape, scratch, mebibytes):
    return pl.pallas_call(
        kernel,
        in_specs=[pl.BlockSpec(memory_space=space) for space in spaces],
        out_specs=[pl.BlockSpec(memory_space=pltpu.VMEM)] * len(out_shape),
        scratch_shapes=scratch,
        out_shape=out_shape,
        compiler_params=pltpu.CompilerParams(vmem_limit_bytes=mebibytes * 1024 * 1024),
    )(*(pltpu.with_memory_space_constraint(o, s) for o, s in zip(operands, spaces)))


def products(ff_blocks, layer_active, x, m):
    hbm, vmem, sems = pltpu.HBM, pltpu.VMEM, pltpu.SemaphoreType.DMA
    pieces = [vmem((2, 2, 2, rows, LANES), jnp.float32) for rows, _ in PAIRS for _ in range(2)]
    tiles = vmem((4, LIVE, 256, 4 * LANES), jnp.bfloat16)
    halves = [vmem((2, 2, 2, 2, rows, LANES), jnp.float32) for rows, _ in PAIRS]
    sent, x_other, x_own, turned = call(
        sent_kernel,
        (ff_blocks, layer_active, x, m),
        (hbm, hbm, hbm, hbm),
        halves[:1] + [tiles, tiles, vmem((m.shape[2], LIVE * 256), jnp.bfloat16)],
        [
            pltpu.SMEM((4,), jnp.int32),
            pltpu.SMEM((4,), jnp.int32),
            sems((2,)),
            sems((4,)),
            sems((4,)),
            vmem(m.shape, jnp.bfloat16),
            sems,
        ],
        6,
    )

    def next_sent(tie):
        return call(next_kernel, (tie(turned), x_other), (vmem, vmem), halves[1:], [], 4)[0]

    def rest(tie):
        return call(
            rest_kernel,
            (tie(turned), x_other, x_own),
            (vmem, vmem, vmem),
            [vmem((FLAT[-1], LANES), jnp.float32)] + pieces + pieces,
            [],
            6,
        )

    return sent, next_sent, rest


def sum_kernel(*refs):
    owns, others, outs = refs[:STREAMS], refs[STREAMS:-STREAMS], refs[-STREAMS:]
    for n, (own, out) in enumerate(zip(owns, outs)):
        def step(k, _):
            at = k // 4, k // 2 % 2, k % 2
            out[at] = own[at] + others[n // 2][(n % 2, *at)]
            return 0

        lax.fori_loop(0, 8, step, 0)


def sums(owns, others):
    return pl.pallas_call(
        sum_kernel,
        in_specs=[pl.BlockSpec(memory_space=pltpu.VMEM)] * (len(owns) + len(others)),
        out_specs=[pl.BlockSpec(memory_space=pltpu.VMEM)] * STREAMS,
        out_shape=[pltpu.VMEM(o.shape, o.dtype) for o in owns],
        input_output_aliases={n: n for n in range(STREAMS)},
        compiler_params=pltpu.CompilerParams(vmem_limit_bytes=2 * 1024 * 1024),
    )(*(pltpu.with_memory_space_constraint(o, pltpu.VMEM) for o in (*owns, *others)))


class Stream:
    def __init__(self, steps):
        self.steps, self.at = steps, 0
        self.send = self.keep = self.flying = None


class Line:
    def __init__(self, token):
        self.token = token

    def tie(self, *values):
        *values, self.token = lax.optimization_barrier((*values, self.token))
        return values[0] if len(values) == 1 else values

    def keep(self, stream, own, other):
        stream.keep = self.token = self.tie(own + other)
        stream.keep = [stream.keep]

    def start(self, stream):
        axis, mask = stream.steps[stream.at]
        self.token = send = self.tie(stream.send)
        stream.flying = swap(send, axis, mask)
        stream.at += 1

    def end(self, stream):
        parts = stream.keep + [self.tie(stream.flying)]
        if stream.at < len(stream.steps):
            stream.send = self.token = self.tie(sum(p[0] for p in parts[1:]) + parts[0][0])
            stream.keep = [p[1] for p in parts]
        else:
            stream.send = self.token = self.tie(sum(parts[1:]) + parts[0])


def message_kernel(*refs):
    *parts, out = refs
    total = sum(jnp.sum((p[...] * p[...]).reshape(-1, 8, LANES), axis=0) for p in parts)
    total = jnp.sum(jnp.sum(total, axis=0, keepdims=True), axis=1, keepdims=True)
    out[...] = jnp.broadcast_to(total[None], out.shape)


def message(parts):
    devices = math.prod(SIZES[a] for a in DP)
    return pl.pallas_call(
        message_kernel,
        in_specs=[pl.BlockSpec(memory_space=pltpu.VMEM)] * len(parts),
        out_specs=pl.BlockSpec(memory_space=pltpu.VMEM),
        out_shape=jax.ShapeDtypeStruct((devices, 1, LANES), jnp.float32),
        compiler_params=pltpu.CompilerParams(vmem_limit_bytes=2 * 1024 * 1024),
    )(*parts)


def shards(inputs, gate_cotangent, ff_blocks, layer_active, param, moment, second_moment):
    sent, next_sent, rest = products(ff_blocks, layer_active, inputs, gate_cotangent)
    flying, firsts, line = {}, None, Line(sent)
    streams = {(n, half): Stream(pair[1][half]) for n, pair in enumerate(PAIRS) for half in range(2)}
    for act, *names in (event.split(":") for event in ORDER):
        if act == "rest":
            other_kept, *owns = rest(line.tie)
            line.token = owns[0]
            continue
        if act == "kept":
            line.token = line.tie(other_kept)
            flat = line.tie(swap(line.token, "core", 1))
            continue
        if act == "sent":
            n = int(names[0])
            line.token = line.tie(sent if n == 0 else next_sent(line.tie))
            flying[n] = swap(line.token, "core", 1)
            continue
        n, half = (int(c) for c in names[0])
        if act == "first":
            if not firsts:
                others = [line.tie(f) for f in flying.values()]
                firsts = sums(owns[:STREAMS], others)
                line.token = firsts[0]
            streams[n, half].send = firsts[2 * n + half]
        elif act == "keep":
            own = owns[STREAMS + 2 * n + half]
            first = FLAT[n] + half * own.size // LANES
            other = flat[first : first + own.size // LANES].reshape(own.shape)
            line.keep(streams[n, half], own, other)
        else:
            getattr(line, act)(streams[n, half])
    done = [stream.send for stream in streams.values()]
    squares = jnp.sum(lax.all_to_all(message(done), DP, 0, 0, tiled=True), axis=0)
    blocks = jnp.concatenate(done, axis=0).T.reshape(8, -1, gate_cotangent.shape[2])
    beside = jnp.broadcast_to(squares[None], blocks.shape[:2] + (LANES,))
    blocks = lax.all_to_all(jnp.concatenate([blocks, beside], axis=2), MP, 0, 0, tiled=True)
    total = jnp.sqrt(jnp.sum(blocks[:, :, -LANES : 1 - LANES], axis=0))
    gradient = blocks[:, :, :-LANES].transpose(1, 0, 2).reshape(param.shape)
    factor = jnp.minimum(1.0, math.sqrt(1.0 * D * FF) / (total + 1e-06))
    clipped = gradient * factor
    new_moment = 0.9 * moment + 0.1 * clipped
    new_second = 0.95 * second_moment + 0.05 * clipped * clipped
    first_hat = new_moment / (1.0 - 0.9**STEP)
    second_hat = new_second / (1.0 - 0.95**STEP)
    new_param = param - 0.02 * (first_hat / (jnp.sqrt(second_hat) + 1e-08) + 0.1 * param)
    return (new_param, new_moment, new_second)


def solution(mesh):
    split = Mesh(mesh.devices.reshape(4, 4, 2, 2, 4), AXES)
    rows = P(AXES, None)
    return jax.shard_map(
        shards,
        mesh=split,
        in_specs=(P(None, DP, None), P(None, DP, MP), P(), P(), rows, rows, rows),
        out_specs=(rows, rows, rows),
        check_vma=False,
    )
```

```python
import functools
import math

import jax
import jax.numpy as jnp
from jax import lax
from jax.experimental import pallas as pl
from jax.experimental.pallas import tpu as pltpu
from jax.sharding import Mesh
from jax.sharding import PartitionSpec as P

D = 4096
FF = 6144
BLOCK = 128
STEP = 10
LANES = 128
LIVE = 3
AXES = ("y", "z", "core", "z_lo", "x")
DP = ("y", "z", "core")
MP = ("z_lo", "x")
SIZES = {"y": 4, "z": 4, "core": 2, "z_lo": 2, "x": 4}

PAIRS = (
    (256, ((("y", 1), ("y", 3), ("z", 1), ("z", 3)), (("y", 3), ("y", 1), ("z", 3), ("z", 1)))),
    (128, ((("z", 1), ("z", 3), ("y", 1), ("y", 3)), (("z", 3), ("z", 1), ("y", 3), ("y", 1)))),
)
STREAMS = 2 * len(PAIRS)
FLAT = [sum(16 * rows for rows, _ in PAIRS[:n]) for n in range(len(PAIRS) + 1)]
ORDER = (
    "sent:0", "sent:1", "rest",
    "first:00", "first:01", "first:10", "first:11", "start:00", "start:01", "start:10", "start:11",
    "kept", "keep:00", "keep:01", "end:00", "end:01", "start:00", "start:01",
    "keep:10", "keep:11", "end:10", "start:10", "end:11", "start:11",
    "end:00", "start:00", "end:01", "start:01", "end:10", "start:10", "end:11", "start:11",
    "end:00", "start:00", "end:01", "start:01", "end:10", "start:10", "end:11", "start:11",
    "end:10", "end:11", "end:00", "end:01",
)


def swap(value, axis, mask):
    return lax.ppermute(value, axis, [(i, i ^ mask) for i in range(SIZES[axis])])


def place_of_tile(step, t, core):
    y_off = (1 - step // 2) * 1 ^ (1 - step % 2) * 3
    z_off = (1 - t // 2) * 1 ^ (1 - t % 2) * 3
    y, z = lax.axis_index("y") ^ y_off, lax.axis_index("z") ^ z_off
    return (y * 4 + z) * 2 + core


def multiply(mt_ref, x_buf, stores, ready=lambda i: None, pairs=(0, 1)):
    for i in range(4):
        ready(i)
        runs, first = [], 0
        for n, (rows, kinds) in enumerate(PAIRS):
            for half, steps in enumerate(kinds):
                tiles = []
                for t in range(4):
                    bit = {("y", 1): i // 2, ("y", 3): i % 2, ("z", 1): t // 2, ("z", 3): t % 2}
                    at = [bit[step] for step in steps]
                    if stores[at[0]] and n in pairs:
                        tiles.append((t, at[0], 4 * at[1] + 2 * at[2] + at[3]))
                lanes = [t for t, _, _ in tiles]
                if runs and runs[-1][0] == lanes:
                    runs[-1][1].append((n, half, first, tiles))
                else:
                    runs.append((lanes, [(n, half, first, tiles)]))
                first += rows
        for lanes, members in runs:
            if not lanes:
                continue
            low, high = members[0][2], members[-1][2] + PAIRS[members[-1][0]][0]
            pieces = [x_buf[i, :, :, t * LANES : (t + 1) * LANES] for t in lanes]
            right = x_buf[i] if len(lanes) == 4 else jnp.concatenate(pieces, axis=2)
            total = jnp.dot(
                mt_ref[low:high],
                right.reshape(LIVE * 256, len(lanes) * LANES),
                preferred_element_type=jnp.float32,
            )
            for n, half, first, tiles in members:
                rows = slice(first - low, first - low + PAIRS[n][0])
                for k, (_, kept, place) in enumerate(tiles):
                    stores[kept](n, half, place, total[rows, k * LANES : (k + 1) * LANES])


def into(refs):
    def store(n, half, place, value):
        refs[2 * n + half][place // 4, place // 2 % 2, place % 2] = value

    return store


def into_pair(ref):
    def store(n, half, place, value):
        ref[half, place // 4, place // 2 % 2, place % 2] = value

    return store


def into_flat(ref):
    def store(n, half, place, value):
        rows = PAIRS[n][0]
        first = FLAT[n] + (8 * half + place) * rows
        ref[first : first + rows] = value

    return store


def load_tiles(x_ref, x_buf, x_sem, subnet, s, core):
    for i in range(4):
        for t in range(4):
            column = pl.multiple_of(place_of_tile(i, t, core) * LANES, LANES)
            pltpu.make_async_copy(
                x_ref.at[subnet, :, pl.ds(column, LANES)],
                x_buf.at[i, s, :, pl.ds(t * LANES, LANES)],
                x_sem.at[i],
            ).start()


def await_tiles(x_buf, x_sem, i):
    pltpu.make_async_copy(x_buf.at[i], x_buf.at[i], x_sem.at[i]).wait()


def sent_kernel(ff_hbm, active_hbm, x_ref, m_ref, *refs):
    out, refs = refs[0], refs[1:]
    x_other, x_own, mt_ref, ff_ref, active_ref, sem, x_sem, own_sem, m_buf, m_sem = refs
    numbers = [
        pltpu.make_async_copy(ff_hbm, ff_ref, sem.at[0]),
        pltpu.make_async_copy(active_hbm, active_ref, sem.at[1]),
    ]
    all_m = pltpu.make_async_copy(m_ref, m_buf, m_sem)
    for c in (*numbers, all_m):
        c.start()
    core = lax.axis_index("core")
    load_tiles(x_ref, x_other, x_sem, 0, 0, 1 - core)
    for c in numbers:
        c.wait()
    idle = sum(jnp.where(active_ref[i] == 1, 0, i) for i in range(1, 4))
    live = [s + (s >= idle).astype(jnp.int32) for s in range(LIVE)]
    for s in range(1, LIVE):
        load_tiles(x_ref, x_other, x_sem, live[s], s, 1 - core)
    for s in range(LIVE):
        load_tiles(x_ref, x_own, own_sem, live[s], s, core)
    all_m.wait()
    cols = m_buf.shape[2]
    first = lax.axis_index(MP) * cols
    for s in range(LIVE):
        values = m_buf[live[s]]
        column = first + lax.broadcasted_iota(jnp.int32, values.shape, 1)
        keep = column < BLOCK * ff_ref[live[s]]
        values = jnp.where(keep, values, jnp.zeros_like(values))
        mt_ref[:, s * 256 : (s + 1) * 256] = values.T
    ready = functools.partial(await_tiles, x_other, x_sem)
    multiply(mt_ref, x_other, (into_pair(out), None), ready, pairs=(0,))
    for i in range(4):
        await_tiles(x_own, own_sem, i)


def next_kernel(mt_ref, x_other, out):
    multiply(mt_ref, x_other, (into_pair(out), None), pairs=(1,))


def rest_kernel(mt_ref, x_other, x_own, other_kept, *refs):
    sent, kept = refs[:STREAMS], refs[STREAMS:]
    multiply(mt_ref, x_other, (None, into_flat(other_kept)))
    multiply(mt_ref, x_own, (into(sent), into(kept)))


def call(kernel, operands, spaces, out_shape, scratch, mebibytes):
    return pl.pallas_call(
        kernel,
        in_specs=[pl.BlockSpec(memory_space=space) for space in spaces],
        out_specs=[pl.BlockSpec(memory_space=pltpu.VMEM)] * len(out_shape),
        scratch_shapes=scratch,
        out_shape=out_shape,
        compiler_params=pltpu.CompilerParams(vmem_limit_bytes=mebibytes * 1024 * 1024),
    )(*(pltpu.with_memory_space_constraint(o, s) for o, s in zip(operands, spaces)))


def products(ff_blocks, layer_active, x, m):
    hbm, vmem, sems = pltpu.HBM, pltpu.VMEM, pltpu.SemaphoreType.DMA
    pieces = [vmem((2, 2, 2, rows, LANES), jnp.float32) for rows, _ in PAIRS for _ in range(2)]
    tiles = vmem((4, LIVE, 256, 4 * LANES), jnp.bfloat16)
    halves = [vmem((2, 2, 2, 2, rows, LANES), jnp.float32) for rows, _ in PAIRS]
    sent, x_other, x_own, turned = call(
        sent_kernel,
        (ff_blocks, layer_active, x, m),
        (hbm, hbm, hbm, hbm),
        halves[:1] + [tiles, tiles, vmem((m.shape[2], LIVE * 256), jnp.bfloat16)],
        [
            pltpu.SMEM((4,), jnp.int32),
            pltpu.SMEM((4,), jnp.int32),
            sems((2,)),
            sems((4,)),
            sems((4,)),
            vmem(m.shape, jnp.bfloat16),
            sems,
        ],
        6,
    )

    def next_sent(tie):
        return call(next_kernel, (tie(turned), x_other), (vmem, vmem), halves[1:], [], 4)[0]

    def rest(tie):
        return call(
            rest_kernel,
            (tie(turned), x_other, x_own),
            (vmem, vmem, vmem),
            [vmem((FLAT[-1], LANES), jnp.float32)] + pieces + pieces,
            [],
            6,
        )

    return sent, next_sent, rest


def sum_kernel(*refs):
    owns, others, outs = refs[:STREAMS], refs[STREAMS:-STREAMS], refs[-STREAMS:]
    for n, (own, out) in enumerate(zip(owns, outs)):
        def step(k, _):
            at = k // 4, k // 2 % 2, k % 2
            out[at] = own[at] + others[n // 2][(n % 2, *at)]
            return 0

        lax.fori_loop(0, 8, step, 0)


def sums(owns, others):
    return pl.pallas_call(
        sum_kernel,
        in_specs=[pl.BlockSpec(memory_space=pltpu.VMEM)] * (len(owns) + len(others)),
        out_specs=[pl.BlockSpec(memory_space=pltpu.VMEM)] * STREAMS,
        out_shape=[pltpu.VMEM(o.shape, o.dtype) for o in owns],
        input_output_aliases={n: n for n in range(STREAMS)},
        compiler_params=pltpu.CompilerParams(vmem_limit_bytes=2 * 1024 * 1024),
    )(*(pltpu.with_memory_space_constraint(o, pltpu.VMEM) for o in (*owns, *others)))


class Stream:
    def __init__(self, steps):
        self.steps, self.at = steps, 0
        self.send = self.keep = self.flying = None


class Line:
    def __init__(self, token):
        self.token = token

    def tie(self, *values):
        *values, self.token = lax.optimization_barrier((*values, self.token))
        return values[0] if len(values) == 1 else values

    def keep(self, stream, own, other):
        stream.keep = self.token = self.tie(own + other)
        stream.keep = [stream.keep]

    def start(self, stream):
        axis, mask = stream.steps[stream.at]
        self.token = send = self.tie(stream.send)
        stream.flying = swap(send, axis, mask)
        stream.at += 1

    def end(self, stream):
        parts = stream.keep + [self.tie(stream.flying)]
        if stream.at < len(stream.steps):
            stream.send = self.token = self.tie(sum(p[0] for p in parts[1:]) + parts[0][0])
            stream.keep = [p[1] for p in parts]
        else:
            stream.send = self.token = self.tie(sum(parts[1:]) + parts[0])


def message_kernel(*refs):
    *parts, out = refs
    total = sum(jnp.sum((p[...] * p[...]).reshape(-1, 8, LANES), axis=0) for p in parts)
    total = jnp.sum(jnp.sum(total, axis=0, keepdims=True), axis=1, keepdims=True)
    out[...] = jnp.broadcast_to(total[None], out.shape)


def message(parts):
    devices = math.prod(SIZES[a] for a in DP)
    return pl.pallas_call(
        message_kernel,
        in_specs=[pl.BlockSpec(memory_space=pltpu.VMEM)] * len(parts),
        out_specs=pl.BlockSpec(memory_space=pltpu.VMEM),
        out_shape=jax.ShapeDtypeStruct((devices, 1, LANES), jnp.float32),
        compiler_params=pltpu.CompilerParams(vmem_limit_bytes=2 * 1024 * 1024),
    )(*parts)


def shards(inputs, gate_cotangent, ff_blocks, layer_active, param, moment, second_moment):
    sent, next_sent, rest = products(ff_blocks, layer_active, inputs, gate_cotangent)
    flying, firsts, line = {}, None, Line(sent)
    streams = {(n, half): Stream(pair[1][half]) for n, pair in enumerate(PAIRS) for half in range(2)}
    for act, *names in (event.split(":") for event in ORDER):
        if act == "rest":
            other_kept, *owns = rest(line.tie)
            line.token = owns[0]
            continue
        if act == "kept":
            line.token = line.tie(other_kept)
            flat = line.tie(swap(line.token, "core", 1))
            continue
        if act == "sent":
            n = int(names[0])
            line.token = line.tie(sent if n == 0 else next_sent(line.tie))
            flying[n] = swap(line.token, "core", 1)
            continue
        n, half = (int(c) for c in names[0])
        if act == "first":
            if not firsts:
                others = [line.tie(f) for f in flying.values()]
                firsts = sums(owns[:STREAMS], others)
                line.token = firsts[0]
            streams[n, half].send = firsts[2 * n + half]
        elif act == "keep":
            own = owns[STREAMS + 2 * n + half]
            first = FLAT[n] + half * own.size // LANES
            other = flat[first : first + own.size // LANES].reshape(own.shape)
            line.keep(streams[n, half], own, other)
        else:
            getattr(line, act)(streams[n, half])
    done = [stream.send for stream in streams.values()]
    squares = jnp.sum(lax.all_to_all(message(done), DP, 0, 0, tiled=True), axis=0)
    blocks = jnp.concatenate(done, axis=0).T.reshape(8, -1, gate_cotangent.shape[2])
    beside = jnp.broadcast_to(squares[None], blocks.shape[:2] + (LANES,))
    blocks = lax.all_to_all(jnp.concatenate([blocks, beside], axis=2), MP, 0, 0, tiled=True)
    total = jnp.sqrt(jnp.sum(blocks[:, :, -LANES : 1 - LANES], axis=0))
    gradient = blocks[:, :, :-LANES].transpose(1, 0, 2).reshape(param.shape)
    factor = jnp.minimum(1.0, math.sqrt(1.0 * D * FF) / (total + 1e-06))
    clipped = gradient * factor
    new_moment = 0.9 * moment + 0.1 * clipped
    new_second = 0.95 * second_moment + 0.05 * clipped * clipped
    first_hat = new_moment / (1.0 - 0.9**STEP)
    second_hat = new_second / (1.0 - 0.95**STEP)
    new_param = param - 0.02 * (first_hat / (jnp.sqrt(second_hat) + 1e-08) + 0.1 * param)
    return (new_param, new_moment, new_second)


def solution(mesh):
    split = Mesh(mesh.devices.reshape(4, 4, 2, 2, 4), AXES)
    rows = P(AXES, None)
    return jax.shard_map(
        shards,
        mesh=split,
        in_specs=(P(None, DP, None), P(None, DP, MP), P(), P(), rows, rows, rows),
        out_specs=(rows, rows, rows),
        check_vma=False,
    )
```
